32 devices in a mesh: grp: 2 (over y), ta: 8 (over z, x), au: 2 (over core).
Axes of the slice: x: 2, y: 2, z: 4, core: 2. Of those that a mesh axis runs over, the one named last changes fastest.
Arguments:
- readings: float32 [16, 8, 256], P('grp', 'au', 'ta'), parts along dimension 0, may hold values from -6 to 6
- present: int32 [16, 8, 256], P('grp', 'au', 'ta'), parts along dimension 0, may hold values 0 or 1
- cell_of: int32 [256], P('ta'), may hold values from 0 to 127, as said below
- noise_var: float32 [256], P('ta'), may hold values from 4 to 160
- kappa: float32 [128], replicated, may hold values from 0.05 to 0.25
- speed: float32 [128], replicated, may hold values from -0.2 to 0.2
- process_var: float32 [128], replicated, may hold values from 0.01 to 0.1
- prior_mean: float32 [256], P('grp'), parts along dimension 0, may hold values from -6 to 6
- prior_var: float32 [128], replicated, may hold values from 0.1 to 1
Outputs:
- filtered_mean: float32 [128, 128], P(('grp', 'ta', 'au')), parts along dimension 0
- smoothed_mean: float32 [128, 128], P(('grp', 'ta', 'au')), parts along dimension 0
- smoothed_var: float32 [128, 128], P(('grp', 'ta', 'au')), parts along dimension 0
The draws below stay inside these ranges and needn't reach their ends.
There are 2 independent parts, one for each index of `grp`. The reference program is written for one: setup_inputs(seed, part) draws one part's arguments, and reference() takes and returns one part's arrays. A program takes and returns all parts, laid end to end along the dimension named above; an argument that names none is the same for every part. Nothing has to cross between parts.
Inputs may be any that keep to these rules, and one draw needn't show every extreme that they name: `cell_of`: each sensor observes one cell; several sensors may share a cell.
All inputs are finite; a program needn't handle non-finite values. No bound on the sum of `present` on one device may be relied on, other than what follows from the above.
Results may differ from the reference program's by a relative error of at most 0.0003.
Values sent between devices are 32-bit elements; how exact they have to be, the bound alone decides.
A program may use at most 128 MiB of HBM per device.

```python
import math
import jax
import jax.numpy as jnp
from jax import lax

NS = 128
SENS_DEV = 32
OUTER = 8
INNER = 8
STEPS = 64
SENS = 256


def sensor_rank(key):
    return jax.random.permutation(jax.random.fold_in(key, 7), SENS).astype(jnp.int32)


def draw_cell_of(key, part):
    rank = sensor_rank(key)
    tight_count = min(64, SENS // 2)
    start_cell = jax.random.randint(jax.random.fold_in(key, 11), (), 0, NS).astype(jnp.int32)
    loose_cells = jax.random.randint(jax.random.fold_in(key, 13), (SENS,), 0, NS).astype(jnp.int32)
    tight_cells = (start_cell + rank // 4) % NS
    return jnp.where(rank < tight_count, tight_cells, loose_cells).astype(jnp.int32)


def draw_noise_var(key, part):
    rank = sensor_rank(key)
    tight_count = min(64, SENS // 2)
    clustered = rank < tight_count
    top_loose = 5.0 * SENS_DEV
    first_u = jax.random.uniform(jax.random.fold_in(key, 17), (SENS,), jnp.float32)
    second_u = jax.random.uniform(jax.random.fold_in(key, 19), (SENS,), jnp.float32)
    tight_vals = jnp.exp(math.log(4.0) + (math.log(16.0) - math.log(4.0)) * first_u)
    loose_vals = jnp.exp(math.log(16.0) + (math.log(top_loose) - math.log(16.0)) * second_u)
    return jnp.where(clustered, tight_vals, loose_vals).astype(jnp.float32)


def set_ends(array, stream_key, smallest, high):
    longest = array.shape.index(max(array.shape))
    spots = []
    for shift in (0, 1):
        where = [jax.random.randint(jax.random.fold_in(stream_key, axis), (), 0, length) for axis, length in enumerate(array.shape)]
        where[longest] = (where[longest] + shift) % array.shape[longest]
        spots.append(tuple(where))
    return array.at[spots[0]].set(smallest).at[spots[1]].set(high)


def level_of(key, shape, split, low, top_value):
    level = 1.0
    for position, parts in split:
        steps = jax.random.uniform(jax.random.fold_in(jax.random.fold_in(key, 6), position), (parts,), jnp.float32, low / len(split), top_value / len(split))
        level = level * jnp.repeat(jnp.exp(steps), shape[position] // parts).reshape((-1,) + (1,) * (len(shape) - 1 - position))
    return level


def noise(own_key, dims, deviation, reach, pieces=(), kind=jnp.bfloat16):
    values = jax.random.normal(own_key, dims, jnp.float32) * deviation
    if len(pieces) > 0:
        values = level_of(own_key, dims, pieces, -0.22, 0.18) * values
    return jnp.clip(values, min=-reach, max=reach).astype(kind)


def setup_inputs(seed: int = 0, part: int = 0) -> dict:
    streams_of = jax.random.split(jax.random.key(seed), 10)
    part_splits = jax.random.split(jax.random.fold_in(streams_of[9], part), 10)
    readings = noise(part_splits[0], (OUTER, INNER, SENS), 1.0, 6.0, ((1, 2), (2, 8)), jnp.float32)
    present = set_ends((jax.random.randint(part_splits[1], (OUTER, INNER, SENS), 0, 4) < 3).astype(jnp.int32), jax.random.fold_in(part_splits[1], 1), 0, 1)
    cell_of = draw_cell_of(jax.random.fold_in(streams_of[9], 71), part)
    noise_var = draw_noise_var(jax.random.fold_in(streams_of[9], 71), part)
    kappa = jnp.clip(jnp.exp(jax.random.uniform(streams_of[4], (NS,), jnp.float32, math.log(0.05), math.log(0.25))), 0.05, 0.25)
    speed = jnp.clip(jax.random.uniform(streams_of[5], (NS,), jnp.float32, -0.2, 0.2), -0.2, 0.2)
    process_var = jnp.clip(jnp.exp(jax.random.uniform(streams_of[6], (NS,), jnp.float32, math.log(0.01), math.log(0.1))), 0.01, 0.1)
    prior_mean = noise(part_splits[7], (NS,), 1.0, 6.0, (), jnp.float32)
    prior_var = jnp.clip(jnp.exp(jax.random.uniform(streams_of[8], (NS,), jnp.float32, math.log(0.1), math.log(1.0))), 0.1, 1.0)
    return {"readings": readings, "present": present, "cell_of": cell_of, "noise_var": noise_var, "kappa": kappa, "speed": speed, "process_var": process_var, "prior_mean": prior_mean, "prior_var": prior_var}


HIGHEST = lax.Precision.HIGHEST

def product(left, right):
    return jnp.matmul(left, right, precision=HIGHEST)

def symmetric(matrix):
    return 0.5 * (matrix + jnp.swapaxes(matrix, -1, -2))

def transition(kappa, speed):
    size_state = kappa.shape[0]
    row_ids = jnp.arange(size_state)[:, None]
    col_ids = jnp.arange(size_state)[None, :]
    ahead = (col_ids == (row_ids + 1) % size_state).astype(jnp.float32)
    behind = (col_ids == (row_ids - 1) % size_state).astype(jnp.float32)
    center = (col_ids == row_ids).astype(jnp.float32)
    return center * (1.0 - 2.0 * kappa)[:, None] + ahead * (kappa - 0.5 * speed)[:, None] + behind * (kappa + 0.5 * speed)[:, None]

def predict(mean, covariance, transition_mat, process_var):
    moved_mean = product(transition_mat, mean)
    moved_cov = symmetric(product(product(transition_mat, covariance), transition_mat.T)) + jnp.diag(process_var)
    return (moved_mean, moved_cov)

def update(mean, covariance, lam_row, info_row):
    root_lam = jnp.sqrt(lam_row)
    unit_mat = jnp.eye(mean.shape[0], dtype=jnp.float32)
    inner_mat = unit_mat + root_lam[:, None] * covariance * root_lam[None, :]
    factor = jnp.linalg.cholesky(inner_mat)
    solved = jax.scipy.linalg.cho_solve((factor, True), root_lam[:, None] * covariance)
    new_cov = symmetric(covariance - product(covariance * root_lam[None, :], solved))
    new_mean = mean + product(new_cov, info_row - lam_row * mean)
    return (new_mean, new_cov)

def reference(readings, present, cell_of, noise_var, kappa, speed, process_var, prior_mean, prior_var):
    transition_mat = transition(kappa, speed)
    size_state = kappa.shape[0]
    weight = present.astype(jnp.float32) / noise_var
    weighted = weight * readings
    one_hot = (cell_of[:, None] == jnp.arange(size_state)[None, :]).astype(jnp.float32)
    lam_all = product(weight.reshape(STEPS, SENS), one_hot)
    info_all = product(weighted.reshape(STEPS, SENS), one_hot)

    def forward(carry, inputs):
        mean, covariance = carry
        mean, covariance = predict(mean, covariance, transition_mat, process_var)
        mean, covariance = update(mean, covariance, inputs[0], inputs[1])
        return ((mean, covariance), (mean, covariance))
    start = (prior_mean, jnp.diag(prior_var))
    _, (means, covariances) = lax.scan(forward, start, (lam_all, info_all))

    def backward(carry, inputs):
        smooth_mean, smooth_cov = carry
        mean, covariance = inputs
        pred_mean, pred_cov = predict(mean, covariance, transition_mat, process_var)
        factor = jnp.linalg.cholesky(pred_cov)
        moved = product(transition_mat, covariance)
        gain = jax.scipy.linalg.cho_solve((factor, True), moved).T
        new_mean = mean + product(gain, smooth_mean - pred_mean)
        new_cov = symmetric(covariance + product(product(gain, smooth_cov - pred_cov), gain.T))
        return ((new_mean, new_cov), (new_mean, jnp.diagonal(new_cov)))
    last_state = (means[-1], covariances[-1])
    _, (smoothed, variances) = lax.scan(backward, last_state, (means[:-1], covariances[:-1]), reverse=True)
    smoothed_mean = jnp.concatenate([smoothed, means[-1:]], 0)
    smoothed_var = jnp.concatenate([variances, jnp.diagonal(covariances[-1])[None, :]], 0)
    return (means, smoothed_mean, smoothed_var)
```

```python
import functools

import jax
import jax.numpy as jnp
from jax import lax
from jax.experimental import pallas as pl
from jax.experimental.pallas import tpu as pltpu
from jax.sharding import PartitionSpec as P

HIGHEST = lax.Precision.HIGHEST
PANEL = 32


def mm(a, b):
    return lax.dot_general(
        a, b, (((1,), (0,)), ((), ())), precision=HIGHEST, preferred_element_type=jnp.float32
    )


def mm_nt(a, b):
    return lax.dot_general(
        a, b, (((1,), (1,)), ((), ())), precision=HIGHEST, preferred_element_type=jnp.float32
    )


def mm_tn(a, b):
    return lax.dot_general(
        a, b, (((0,), (0,)), ((), ())), precision=HIGHEST, preferred_element_type=jnp.float32
    )


def eye_mask(n):
    return lax.broadcasted_iota(jnp.int32, (n, n), 0) == lax.broadcasted_iota(
        jnp.int32, (n, n), 1
    )


def diag_of(row):
    n = row.shape[1]
    return jnp.where(eye_mask(n), jnp.broadcast_to(row, (n, n)), 0.0)


def sweep_panels(panels):
    lanes = lax.broadcasted_iota(jnp.int32, panels[0].shape, 1)
    subs = lax.broadcasted_iota(jnp.int32, panels[0].shape, 0)
    row_lanes = lax.broadcasted_iota(jnp.int32, (1, panels[0].shape[1]), 1)
    for j in range(PANEL):
        out = []
        for panel in panels:
            col = panel[:, j : j + 1]
            row = panel[j : j + 1, :]
            inv = 1.0 / panel[j : j + 1, j : j + 1]
            row = jnp.where(row_lanes == j, -1.0, row) * inv
            rest = jnp.where(lanes == j, 0.0, panel)
            out.append(jnp.where(subs == j, row, rest - col * row))
        panels = out
    return panels


def inverses(mats, work):
    n = mats[0].shape[0]
    count = len(mats)
    for i, mat in enumerate(mats):
        work[i] = mat

    def block(_, carry):
        rows = [work[i, :PANEL, :] for i in range(count)]
        swept = sweep_panels(rows)
        lanes = lax.broadcasted_iota(jnp.int32, (PANEL, n), 1)
        for i in range(count):
            cross = jnp.where(lanes < PANEL, 0.0, rows[i])
            low = work[i, PANEL:, :]
            low_lanes = lax.broadcasted_iota(jnp.int32, low.shape, 1)
            change = mm_tn(cross, swept[i])
            low = jnp.where(low_lanes < PANEL, 0.0, low) - change[PANEL:, :]
            work[i, : n - PANEL, :] = pltpu.roll(low, n - PANEL, 1)
            work[i, n - PANEL :, :] = pltpu.roll(swept[i], n - PANEL, 1)
        return carry

    lax.fori_loop(0, n // PANEL, block, 0)
    return [-work[i] for i in range(count)]


def middle(first, second):
    return first[2] + second[0]


def joined(first, second, inv):
    e1, g1, _, v1, w1 = first
    _, g2, h2, v2, w2 = second
    u = mm(w1 + v2, inv)
    left = mm(g1, inv)
    right = mm(inv, g2)
    return (
        e1 - mm_nt(left, g1),
        mm(left, g2),
        h2 - mm_tn(g2, right),
        v1 + mm_nt(u, g1),
        w2 + mm(u, g2),
    )


def joined_high(first, second, inv):
    _, g2, h2, v2, w2 = second
    u = mm(first[4] + v2, inv)
    return h2 - mm_tn(g2, mm(inv, g2)), w2 + mm(u, g2)


def joined_low(first, second, inv):
    e1, g1, _, v1, w1 = first
    u = mm(w1 + second[3], inv)
    return e1 - mm_nt(mm(g1, inv), g1), v1 + mm_nt(u, g1)


def put(ref, at, element):
    n = element[0].shape[0]
    ref[at, 0:n, :] = element[0]
    ref[at, n : 2 * n, :] = element[1]
    ref[at, 2 * n : 3 * n, :] = element[2]
    ref[at, 3 * n : 3 * n + 1, :] = element[3]
    ref[at, 3 * n + 1 : 3 * n + 2, :] = element[4]
    ref[at, 3 * n + 2 : 3 * n + 8, :] = jnp.zeros((6, n), jnp.float32)


def get(ref, at):
    n = ref.shape[2]
    return (
        ref[at, 0:n, :],
        ref[at, n : 2 * n, :],
        ref[at, 2 * n : 3 * n, :],
        ref[at, 3 * n : 3 * n + 1, :],
        ref[at, 3 * n + 1 : 3 * n + 2, :],
    )


def first_kernel(cov_ref, out_ref, work):
    out_ref[...] = inverses([cov_ref[...]], work)[0]


def local_kernel(place_ref, data_ref, trans_ref, g_ref, e_ref, q_ref, first_ref, prior_ref,
                 locals_ref, agg_ref, work):
    n = trans_ref.shape[0]
    steps = (data_ref.shape[0] - 1) // 2
    trans = trans_ref[...]
    pull = g_ref[...]
    curv = e_ref[...]
    var = q_ref[...]
    is_first = place_ref[0] == 0
    is_last = place_ref[0] == place_ref[1] - 1
    cells = data_ref[2 * steps : 2 * steps + 1, :]
    sensors = cells.shape[1]
    states = lax.broadcasted_iota(jnp.int32, (n, sensors), 0).astype(jnp.float32)
    one_hot = jnp.where(states == cells, 1.0, 0.0)
    sums = mm_nt(data_ref[0 : 2 * steps, :], one_hot)
    zero = jnp.zeros((n, n), jnp.float32)
    zero_row = jnp.zeros((1, n), jnp.float32)
    single = []
    for t in range(steps):
        lam, info = sums[t : t + 1, :], sums[steps + t : steps + t + 1, :]
        single.append((curv, pull, diag_of(1.0 / var + lam), zero_row, info))
    lam, info = sums[0:1, :], sums[steps : steps + 1, :]
    moved = mm_nt(prior_ref[...], trans)
    known = first_ref[...]
    head = (zero, zero, known + diag_of(lam), zero_row, info + mm(moved, known))
    single[0] = tuple(jnp.where(is_first, a, b) for a, b in zip(head, single[0]))
    lam, info = sums[steps - 1 : steps, :], sums[2 * steps - 1 : 2 * steps, :]
    damp = 1.0 / (1.0 + var * lam)
    tail = (
        mm_tn(trans, mm(diag_of(lam * damp), trans)), zero, zero,
        mm(info * damp, trans), zero_row,
    )
    tail = tuple(jnp.where(is_last, a, b) for a, b in zip(tail, single[3]))
    s0, s1, s2, s3 = single
    m01, m23, m23t = inverses([middle(s0, s1), middle(s2, s3), middle(s2, tail)], work)
    s01 = joined(s0, s1, m01)
    s23 = joined(s2, s3, m23)
    s23t = joined(s2, tail, m23t)
    put(locals_ref, 0, s0)
    put(locals_ref, 1, s01)
    put(locals_ref, 5, s23)
    put(locals_ref, 6, s3)
    pairs = [(s01, s2), (s01, s23), (s1, s23), (s01, s23t)]
    found = inverses([middle(a, b) for a, b in pairs], work)
    for slot, (a, b), inv in zip((2, 3, 4), pairs, found):
        put(locals_ref, slot, joined(a, b, inv))
    put(agg_ref, 0, joined(*pairs[3], found[3]))


def level_kernel(level, last, place_ref, own_ref, other_ref, sides_ref, agg_ref, out_ref, work):
    n = own_ref.shape[2]
    place = place_ref[0]
    span = 1 << level
    upper = (place // span) % 2 == 1
    inside = place % span
    own, other = get(own_ref, 0), get(other_ref, 0)

    def pick(a, b):
        return tuple(jnp.where(upper, x, y) for x, y in zip(a, b))

    wanted = []
    if not last:
        low, high = pick(other, own), pick(own, other)
        wanted.append(middle(low, high))
    if level > 0:
        before, after = get(sides_ref, 0), get(sides_ref, 1)
        alone = jnp.where(upper, inside == 0, inside == span - 1)
        one, two = pick(other, after), pick(before, other)
        unit = jnp.where(eye_mask(n), 1.0, 0.0)
        wanted.append(jnp.where(alone, unit, middle(one, two)))
    found = inverses(wanted, work)
    if not last:
        put(agg_ref, 0, joined(low, high, found[0]))
    if level > 0:
        merged = joined(one, two, found[-1])
        merged = tuple(jnp.where(alone, x, y) for x, y in zip(other, merged))
        put(out_ref, 0, pick(merged, before))
        put(out_ref, 1, pick(after, merged))
    else:
        empty = tuple(jnp.zeros_like(x) for x in other)
        put(out_ref, 0, pick(other, empty))
        put(out_ref, 1, pick(empty, other))


def final_kernel(place_ref, locals_ref, sides_ref, mean_ref, smooth_ref, var_ref, work):
    n = locals_ref.shape[2]
    is_first = place_ref[0] == 0
    unit = jnp.where(eye_mask(n), 1.0, 0.0)
    before = list(get(sides_ref, 0))
    before[2] = jnp.where(is_first, unit, before[2])
    after = get(sides_ref, 1)
    ahead = [get(locals_ref, i) for i in range(4)]
    behind = [get(locals_ref, i) for i in range(4, 7)]
    found = inverses(
        [middle(before, a) for a in ahead] + [middle(b, after) for b in behind], work
    )
    states = [joined_high(before, a, inv) for a, inv in zip(ahead, found[:4])]
    later = [joined_low(b, after, inv) for b, inv in zip(behind, found[4:])]
    later.append((after[0], after[3]))
    found = inverses(
        [s[0] for s in states] + [s[0] + l[0] for s, l in zip(states, later)], work
    )
    diagonal = eye_mask(n)
    for t in range(4):
        mean_ref[t : t + 1, :] = mm(states[t][1], found[t])
        smooth_ref[t : t + 1, :] = mm(states[t][1] + later[t][1], found[4 + t])
        var_ref[t : t + 1, :] = jnp.sum(
            jnp.where(diagonal, found[4 + t], 0.0), axis=0, keepdims=True
        )


def run(kernel, shapes, works, operands, n, scalars=1):
    specs = [pl.BlockSpec(memory_space=pltpu.SMEM)] * scalars
    specs += [pl.BlockSpec(memory_space=pltpu.VMEM)] * (len(operands) - scalars)
    single = not isinstance(shapes, list)
    outs = pl.BlockSpec(memory_space=pltpu.VMEM)
    return pl.pallas_call(
        kernel,
        out_shape=shapes,
        in_specs=specs,
        out_specs=outs if single else [outs] * len(shapes),
        scratch_shapes=[pltpu.VMEM((works, n, n), jnp.float32)],
        compiler_params=pltpu.CompilerParams(vmem_limit_bytes=40 * 2**20),
    )(*operands)


def transition(kappa, speed):
    n = kappa.shape[0]
    rows = jnp.arange(n)[:, None]
    cols = jnp.arange(n)[None, :]
    ahead = (cols == (rows + 1) % n).astype(jnp.float32)
    behind = (cols == (rows - 1) % n).astype(jnp.float32)
    center = (cols == rows).astype(jnp.float32)
    return (
        center * (1.0 - 2.0 * kappa)[:, None]
        + ahead * (kappa - 0.5 * speed)[:, None]
        + behind * (kappa + 0.5 * speed)[:, None]
    )


def local(readings, present, cell_of, noise_var, kappa, speed, process_var, prior_mean, prior_var):
    n = kappa.shape[0]
    outer, steps, sensors = readings.shape
    blocks = lax.axis_size("ta") * lax.axis_size("au")
    place = lax.axis_index("ta") * lax.axis_size("au") + lax.axis_index("au")
    where = jnp.stack([place, jnp.full_like(place, blocks)]).astype(jnp.int32)
    weight = present.astype(jnp.float32) / noise_var
    cells = jnp.broadcast_to(cell_of.astype(jnp.float32), (outer, 1, sensors))
    sent = jnp.concatenate([weight, weight * readings, cells], axis=1)
    data = lax.all_to_all(sent, "ta", split_axis=0, concat_axis=0, tiled=True)
    data = jnp.swapaxes(data, 0, 1).reshape(2 * steps + 1, outer * sensors)

    trans = transition(kappa, speed)
    pull = trans.T / process_var[None, :]
    curv = jnp.matmul(pull, trans, precision=HIGHEST)
    start = jnp.matmul(trans * prior_var[None, :], trans.T, precision=HIGHEST)
    start = start + jnp.diag(process_var)
    mat = jax.ShapeDtypeStruct((n, n), jnp.float32)
    known = run(first_kernel, mat, 1, [start], n, 0)

    def elements(count):
        return jax.ShapeDtypeStruct((count, 3 * n + 8, n), jnp.float32)

    pieces, agg = run(
        local_kernel, [elements(7), elements(1)], 4,
        [where, data, trans, pull, curv, process_var[None, :], known, prior_mean[None, :]], n,
    )
    sides = jnp.zeros((2, 3 * n + 8, n), jnp.float32)
    levels = blocks.bit_length() - 1
    for level in range(levels):
        pairs = [(i, i ^ (1 << level)) for i in range(blocks)]
        other = lax.ppermute(agg, ("ta", "au"), pairs)
        agg, sides = run(
            functools.partial(level_kernel, level, level == levels - 1),
            [elements(1), elements(2)], 2, [where, agg, other, sides], n,
        )
    row = jax.ShapeDtypeStruct((steps, n), jnp.float32)
    return tuple(run(final_kernel, [row, row, row], 8, [where, pieces, sides], n))


def solution(mesh):
    placed = (
        P("grp", "au", "ta"),
        P("grp", "au", "ta"),
        P("ta"),
        P("ta"),
        P(),
        P(),
        P(),
        P("grp"),
        P(),
    )
    out = P(("grp", "ta", "au"), None)
    return jax.shard_map(
        local, mesh=mesh, in_specs=placed, out_specs=(out, out, out), check_vma=False
    )
```

```python
import functools

import jax
import jax.numpy as jnp
from jax import lax
from jax.experimental import pallas as pl
from jax.experimental.pallas import tpu as pltpu
from jax.sharding import PartitionSpec as P

HIGHEST = lax.Precision.HIGHEST
PANEL = 32


def mm(a, b):
    return lax.dot_general(
        a, b, (((1,), (0,)), ((), ())), precision=HIGHEST, preferred_element_type=jnp.float32
    )


def mm_nt(a, b):
    return lax.dot_general(
        a, b, (((1,), (1,)), ((), ())), precision=HIGHEST, preferred_element_type=jnp.float32
    )


def mm_tn(a, b):
    return lax.dot_general(
        a, b, (((0,), (0,)), ((), ())), precision=HIGHEST, preferred_element_type=jnp.float32
    )


def eye_mask(n):
    return lax.broadcasted_iota(jnp.int32, (n, n), 0) == lax.broadcasted_iota(
        jnp.int32, (n, n), 1
    )


def diag_of(row):
    n = row.shape[1]
    return jnp.where(eye_mask(n), jnp.broadcast_to(row, (n, n)), 0.0)


def four_rows(panel, j):
    rows, n = panel.shape
    row_lanes = lax.broadcasted_iota(jnp.int32, (1, n), 1)
    cols = [jnp.broadcast_to(panel[:, j + m : j + m + 1], (rows, n)) for m in range(4)]
    d = [[cols[m][j + i : j + i + 1, :] for m in range(4)] for i in range(4)]
    r = []
    for i in range(4):
        row = jnp.where((row_lanes >= j) & (row_lanes < j + 4), 0.0, panel[j + i : j + i + 1, :])
        r.append(jnp.where(row_lanes == j + i, -1.0, row))
    inv = 1.0 / (d[0][0] * d[1][1] - d[1][0] * d[1][0])
    a0, a1, a2 = d[1][1] * inv, d[1][0] * inv, d[0][0] * inv
    x20, x21 = d[2][0] * a0 - d[2][1] * a1, d[2][1] * a2 - d[2][0] * a1
    x30, x31 = d[3][0] * a0 - d[3][1] * a1, d[3][1] * a2 - d[3][0] * a1
    s22 = d[2][2] - (x20 * d[2][0] + x21 * d[2][1])
    s23 = d[3][2] - (x20 * d[3][0] + x21 * d[3][1])
    s33 = d[3][3] - (x30 * d[3][0] + x31 * d[3][1])
    inv = 1.0 / (s22 * s33 - s23 * s23)
    y2 = r[2] - (x20 * r[0] + x21 * r[1])
    y3 = r[3] - (x30 * r[0] + x31 * r[1])
    w2 = inv * (s33 * y2 - s23 * y3)
    w3 = inv * (s22 * y3 - s23 * y2)
    w0 = (a0 * r[0] - a1 * r[1]) - (x20 * w2 + x30 * w3)
    w1 = (a2 * r[1] - a1 * r[0]) - (x21 * w2 + x31 * w3)
    return cols, [w0, w1, w2, w3]


def sweep_panels(panels):
    lanes = lax.broadcasted_iota(jnp.int32, panels[0].shape, 1)
    subs = lax.broadcasted_iota(jnp.int32, panels[0].shape, 0)
    for j in range(0, PANEL, 4):
        found = [four_rows(panel, j) for panel in panels]
        out = []
        for panel, (cols, w) in zip(panels, found):
            new = jnp.where((lanes >= j) & (lanes < j + 4), 0.0, panel)
            new = new - ((cols[0] * w[0] + cols[1] * w[1]) + (cols[2] * w[2] + cols[3] * w[3]))
            for m in range(4):
                new = jnp.where(subs == j + m, w[m], new)
            out.append(new)
        panels = out
    return panels


def inverses(mats, work):
    n = mats[0].shape[0]
    count = len(mats)
    for i, mat in enumerate(mats):
        work[i] = mat

    def block(_, carry):
        rows = [work[i, :PANEL, :] for i in range(count)]
        swept = sweep_panels(rows)
        lanes = lax.broadcasted_iota(jnp.int32, (PANEL, n), 1)
        for i in range(count):
            cross = jnp.where(lanes < PANEL, 0.0, rows[i])
            low = work[i, PANEL:, :]
            low_lanes = lax.broadcasted_iota(jnp.int32, low.shape, 1)
            change = mm_tn(cross, swept[i])
            low = jnp.where(low_lanes < PANEL, 0.0, low) - change[PANEL:, :]
            work[i, : n - PANEL, :] = pltpu.roll(low, n - PANEL, 1)
            work[i, n - PANEL :, :] = pltpu.roll(swept[i], n - PANEL, 1)
        return carry

    lax.fori_loop(0, n // PANEL, block, 0)
    return [-work[i] for i in range(count)]


def middle(spread, curv):
    return spread + mm(mm(spread, curv), spread)


def joined_with(first, second, left, mid, y):
    e1, a1, _, p1, _ = first
    e2, a2, c2, p2, b2 = second
    return (
        e1 + mm_tn(a1, mm(mm(e2, left), a1)),
        mm(mm(a2, left), a1),
        c2 + mm_nt(mm(a2, mid), a2),
        p1 + mm(p2 - mm(y, e2), a1),
        b2 + mm_nt(y, a2),
    )


def joined(first, second, inv):
    c1 = first[2]
    left = mm(c1, inv)
    y = mm_nt(first[4] + mm(second[3], c1), left)
    return joined_with(first, second, left, mm(left, c1), y)


def joined_step(first, info, scale, second, inv):
    return joined_with(first, second, inv * scale, inv, mm(info + second[3], inv))


def joined_high(first, second, inv):
    c1 = first[2]
    _, a2, c2, p2, b2 = second
    left = mm(c1, inv)
    y = mm_nt(first[4] + mm(p2, c1), left)
    return c2 + mm_nt(mm(a2, mm(left, c1)), a2), b2 + mm_nt(y, a2)


def joined_low(first, second, inv):
    e1, a1, c1, p1, b1 = first
    e2, p2 = second[0], second[3]
    left = mm(c1, inv)
    y = mm_nt(b1 + mm(p2, c1), left)
    return e1 + mm_tn(a1, mm(mm(e2, left), a1)), p1 + mm(p2 - mm(y, e2), a1)


def put(ref, at, element):
    n = element[0].shape[0]
    ref[at, 0:n, :] = element[0]
    ref[at, n : 2 * n, :] = element[1]
    ref[at, 2 * n : 3 * n, :] = element[2]
    ref[at, 3 * n : 3 * n + 1, :] = element[3]
    ref[at, 3 * n + 1 : 3 * n + 2, :] = element[4]
    ref[at, 3 * n + 2 : 3 * n + 8, :] = jnp.zeros((6, n), jnp.float32)


def get(ref, at):
    n = ref.shape[2]
    return (
        ref[at, 0:n, :],
        ref[at, n : 2 * n, :],
        ref[at, 2 * n : 3 * n, :],
        ref[at, 3 * n : 3 * n + 1, :],
        ref[at, 3 * n + 1 : 3 * n + 2, :],
    )


def first_kernel(cov_ref, out_ref, work):
    out_ref[...] = inverses([cov_ref[...]], work)[0]


def local_kernel(place_ref, data_ref, trans_ref, q_ref, first_ref, prior_ref,
                 locals_ref, agg_ref, work):
    n = trans_ref.shape[0]
    steps = (data_ref.shape[0] - 1) // 2
    trans = trans_ref[...]
    var = q_ref[...]
    is_first = place_ref[0] == 0
    is_last = place_ref[0] == place_ref[1] - 1
    cells = data_ref[2 * steps : 2 * steps + 1, :]
    sensors = cells.shape[1]
    states = lax.broadcasted_iota(jnp.int32, (n, sensors), 0).astype(jnp.float32)
    one_hot = jnp.where(states == cells, 1.0, 0.0)
    sums = mm_nt(data_ref[0 : 2 * steps, :], one_hot)
    zero = jnp.zeros((n, n), jnp.float32)
    zero_row = jnp.zeros((1, n), jnp.float32)
    single, infos, scales = [], [], []
    for t in range(steps):
        lam, info = sums[t : t + 1, :], sums[steps + t : steps + t + 1, :]
        damp = 1.0 / (1.0 + var * lam)
        shrink = var * damp
        single.append((
            mm_tn(trans, mm(diag_of(lam * damp), trans)), mm(diag_of(damp), trans),
            diag_of(shrink), mm(info * damp, trans), shrink * info,
        ))
        infos.append(info)
        scales.append(1.0 / var + lam)
    known = first_ref[...]
    moved = mm_nt(prior_ref[...], trans)
    known_info = infos[0] + mm(moved, known)
    info0 = jnp.where(is_first, known_info, infos[0])
    high0 = jnp.where(is_first, known + diag_of(sums[0:1, :]), diag_of(scales[0]))
    e3, _, _, p3, _ = single[3]
    tail = tuple(
        jnp.where(is_last, a, b) for a, b in zip((e3, zero, zero, p3, zero_row), single[3])
    )
    s0, s1, s2, s3 = single
    m0, m01, m23 = inverses([high0, high0 + s1[0], diag_of(scales[2]) + s3[0]], work)
    head = (zero, zero, m0, zero_row, mm(info0, m0))
    s0 = tuple(jnp.where(is_first, a, b) for a, b in zip(head, s0))
    s01 = joined_step(s0, info0, scales[0], s1, m01)
    s23 = joined_step(s2, infos[2], scales[2], s3, m23)
    s23t = joined_step(s2, infos[2], scales[2], tail, m23)
    put(locals_ref, 0, s0)
    put(locals_ref, 1, s01)
    put(locals_ref, 5, s23)
    put(locals_ref, 6, s3)
    found = inverses(
        [middle(s01[2], s2[0]), middle(s01[2], s23[0]), diag_of(scales[1]) + s23[0]], work
    )
    put(locals_ref, 2, joined(s01, s2, found[0]))
    put(locals_ref, 3, joined(s01, s23, found[1]))
    put(locals_ref, 4, joined_step(s1, infos[1], scales[1], s23, found[2]))
    put(agg_ref, 0, joined(s01, s23t, found[1]))


def level_kernel(level, narrow, place_ref, own_ref, other_ref, sides_ref, agg_ref, out_ref, work):
    n = own_ref.shape[2]
    place = place_ref[0]
    span = 1 << level
    upper = (place // span) % 2 == 1
    inside = place % span
    own, other = get(own_ref, 0), get(other_ref, 0)

    def pick(a, b):
        return tuple(jnp.where(upper, x, y) for x, y in zip(a, b))

    low, high = pick(other, own), pick(own, other)
    wanted = [middle(low[2], high[0])]
    if level > 0:
        before, after = get(sides_ref, 0), get(sides_ref, 1)
        alone = jnp.where(upper, inside == 0, inside == span - 1)
        one, two = pick(other, after), pick(before, other)
        unit = jnp.where(eye_mask(n), 1.0, 0.0)
        wanted.append(jnp.where(alone, unit, middle(one[2], two[0])))
    found = inverses(wanted, work)
    agg = joined(low, high, found[0])
    if narrow:
        above = (place // (2 * span)) % 2 == 1
        agg_ref[0:n, :] = jnp.where(above, agg[0], agg[2])
        agg_ref[n : n + 1, :] = jnp.where(above, agg[3], agg[4])
        agg_ref[n + 1 : n + 8, :] = jnp.zeros((7, n), jnp.float32)
    else:
        put(agg_ref, 0, agg)
    if level > 0:
        merged = joined(one, two, found[-1])
        merged = tuple(jnp.where(alone, x, y) for x, y in zip(other, merged))
        put(out_ref, 0, pick(merged, before))
        put(out_ref, 1, pick(after, merged))
    else:
        empty = tuple(jnp.zeros_like(x) for x in other)
        put(out_ref, 0, pick(other, empty))
        put(out_ref, 1, pick(empty, other))


def last_level(place, span, other_ref, sides_ref, work):
    n = other_ref.shape[1]
    upper = (place // span) % 2 == 1
    inside = place % span
    alone = jnp.where(upper, inside == 0, inside == span - 1)
    before, after = get(sides_ref, 0), get(sides_ref, 1)
    mat, vec = other_ref[0:n, :], other_ref[n : n + 1, :]
    unit = jnp.where(eye_mask(n), 1.0, 0.0)
    c1 = jnp.where(upper, mat, after[2])
    e2 = jnp.where(upper, before[0], mat)
    b1 = jnp.where(upper, vec, after[4])
    p2 = jnp.where(upper, before[3], vec)
    inv = inverses([jnp.where(alone, unit, middle(c1, e2))], work)[0]
    left = mm(c1, inv)
    y = mm_nt(b1 + mm(p2, c1), left)
    link = jnp.where(upper, before[1].T, after[1])
    core = jnp.where(upper, mm(left, c1), mm(e2, left))
    y = jnp.where(upper, y, p2 - mm(y, e2))
    new = jnp.where(upper, before[2], after[0]) + mm_tn(link, mm(core, link))
    row = jnp.where(upper, before[4], after[3]) + mm(y, link)
    new, row = jnp.where(alone, mat, new), jnp.where(alone, vec, row)
    before = (None, None, jnp.where(upper, new, before[2]), None, jnp.where(upper, row, before[4]))
    after = (jnp.where(upper, after[0], new), None, None, jnp.where(upper, after[3], row), None)
    return before, after


def final_kernel(span, place_ref, locals_ref, other_ref, sides_ref, mean_ref, smooth_ref, var_ref, work):
    n = locals_ref.shape[2]
    is_first = place_ref[0] == 0
    unit = jnp.where(eye_mask(n), 1.0, 0.0)
    before, after = last_level(place_ref[0], span, other_ref, sides_ref, work)
    before = (None, None, jnp.where(is_first, unit, before[2]), None, before[4])
    ahead = [get(locals_ref, i) for i in range(4)]
    behind = [get(locals_ref, i) for i in range(4, 7)]
    found = inverses(
        [middle(before[2], a[0]) for a in ahead] + [middle(b[2], after[0]) for b in behind], work
    )
    states = [joined_high(before, a, inv) for a, inv in zip(ahead, found[:4])]
    later = [joined_low(b, after, inv) for b, inv in zip(behind, found[4:])]
    later.append((after[0], after[3]))
    found = inverses([middle(s[0], l[0]) for s, l in zip(states, later)], work)
    diagonal = eye_mask(n)
    for t, ((cov, mean), (_, row)) in enumerate(zip(states, later)):
        left = mm(cov, found[t])
        mean_ref[t : t + 1, :] = mean
        smooth_ref[t : t + 1, :] = mm_nt(mean + mm(row, cov), left)
        var_ref[t : t + 1, :] = jnp.sum(
            jnp.where(diagonal, mm(left, cov), 0.0), axis=0, keepdims=True
        )


def run(kernel, shapes, works, operands, n, scalars=1):
    specs = [pl.BlockSpec(memory_space=pltpu.SMEM)] * scalars
    specs += [pl.BlockSpec(memory_space=pltpu.VMEM)] * (len(operands) - scalars)
    single = not isinstance(shapes, list)
    outs = pl.BlockSpec(memory_space=pltpu.VMEM)
    return pl.pallas_call(
        kernel,
        out_shape=shapes,
        in_specs=specs,
        out_specs=outs if single else [outs] * len(shapes),
        scratch_shapes=[pltpu.VMEM((works, n, n), jnp.float32)],
        compiler_params=pltpu.CompilerParams(vmem_limit_bytes=40 * 2**20),
    )(*operands)


def transition(kappa, speed):
    n = kappa.shape[0]
    rows = jnp.arange(n)[:, None]
    cols = jnp.arange(n)[None, :]
    ahead = (cols == (rows + 1) % n).astype(jnp.float32)
    behind = (cols == (rows - 1) % n).astype(jnp.float32)
    center = (cols == rows).astype(jnp.float32)
    return (
        center * (1.0 - 2.0 * kappa)[:, None]
        + ahead * (kappa - 0.5 * speed)[:, None]
        + behind * (kappa + 0.5 * speed)[:, None]
    )


def local(readings, present, cell_of, noise_var, kappa, speed, process_var, prior_mean, prior_var):
    n = kappa.shape[0]
    outer, steps, sensors = readings.shape
    blocks = lax.axis_size("ta") * lax.axis_size("au")
    place = lax.axis_index("ta") * lax.axis_size("au") + lax.axis_index("au")
    where = jnp.stack([place, jnp.full_like(place, blocks)]).astype(jnp.int32)
    weight = present.astype(jnp.float32) / noise_var
    cells = jnp.broadcast_to(cell_of.astype(jnp.float32), (outer, 1, sensors))
    sent = jnp.concatenate([weight, weight * readings, cells], axis=1)
    data = lax.all_to_all(sent, "ta", split_axis=0, concat_axis=0, tiled=True)
    data = jnp.swapaxes(data, 0, 1).reshape(2 * steps + 1, outer * sensors)

    trans = transition(kappa, speed)
    start = jnp.matmul(trans * prior_var[None, :], trans.T, precision=HIGHEST)
    start = start + jnp.diag(process_var)
    mat = jax.ShapeDtypeStruct((n, n), jnp.float32)
    known = run(first_kernel, mat, 1, [start], n, 0)

    def elements(count):
        return jax.ShapeDtypeStruct((count, 3 * n + 8, n), jnp.float32)

    pieces, agg = run(
        local_kernel, [elements(7), elements(1)], 4,
        [where, data, trans, process_var[None, :], known, prior_mean[None, :]], n,
    )
    sides = jnp.zeros((2, 3 * n + 8, n), jnp.float32)
    levels = blocks.bit_length() - 1
    for level in range(levels):
        pairs = [(i, i ^ (1 << level)) for i in range(blocks)]
        other = lax.ppermute(agg, ("ta", "au"), pairs)
        if level == levels - 1:
            break
        narrow = level == levels - 2
        sent = jax.ShapeDtypeStruct((n + 8, n), jnp.float32) if narrow else elements(1)
        agg, sides = run(
            functools.partial(level_kernel, level, narrow),
            [sent, elements(2)], 2, [where, agg, other, sides], n,
        )
    row = jax.ShapeDtypeStruct((steps, n), jnp.float32)
    return tuple(
        run(
            functools.partial(final_kernel, blocks // 2),
            [row, row, row], 8, [where, pieces, other, sides], n,
        )
    )


def solution(mesh):
    placed = (
        P("grp", "au", "ta"),
        P("grp", "au", "ta"),
        P("ta"),
        P("ta"),
        P(),
        P(),
        P(),
        P("grp"),
        P(),
    )
    out = P(("grp", "ta", "au"), None)
    return jax.shard_map(
        local, mesh=mesh, in_specs=placed, out_specs=(out, out, out), check_vma=False
    )
```

```python
import functools

import jax
import jax.numpy as jnp
from jax import lax
from jax.experimental import pallas as pl
from jax.experimental.pallas import tpu as pltpu
from jax.sharding import PartitionSpec as P

HIGHEST = lax.Precision.HIGHEST
PANEL = 32


def mm(a, b):
    return lax.dot_general(
        a, b, (((1,), (0,)), ((), ())), precision=HIGHEST, preferred_element_type=jnp.float32
    )


def mm_nt(a, b):
    return lax.dot_general(
        a, b, (((1,), (1,)), ((), ())), precision=HIGHEST, preferred_element_type=jnp.float32
    )


def mm_tn(a, b):
    return lax.dot_general(
        a, b, (((0,), (0,)), ((), ())), precision=HIGHEST, preferred_element_type=jnp.float32
    )


def eye_mask(n):
    return lax.broadcasted_iota(jnp.int32, (n, n), 0) == lax.broadcasted_iota(
        jnp.int32, (n, n), 1
    )


def diag_of(row):
    n = row.shape[1]
    return jnp.where(eye_mask(n), jnp.broadcast_to(row, (n, n)), 0.0)


def four_rows(panel, j):
    rows, n = panel.shape
    row_lanes = lax.broadcasted_iota(jnp.int32, (1, n), 1)
    cols = [jnp.broadcast_to(panel[:, j + m : j + m + 1], (rows, n)) for m in range(4)]
    d = [[cols[m][j + i : j + i + 1, :] for m in range(4)] for i in range(4)]
    r = []
    for i in range(4):
        row = jnp.where((row_lanes >= j) & (row_lanes < j + 4), 0.0, panel[j + i : j + i + 1, :])
        r.append(jnp.where(row_lanes == j + i, -1.0, row))
    inv = 1.0 / (d[0][0] * d[1][1] - d[1][0] * d[1][0])
    a0, a1, a2 = d[1][1] * inv, d[1][0] * inv, d[0][0] * inv
    x20, x21 = d[2][0] * a0 - d[2][1] * a1, d[2][1] * a2 - d[2][0] * a1
    x30, x31 = d[3][0] * a0 - d[3][1] * a1, d[3][1] * a2 - d[3][0] * a1
    s22 = d[2][2] - (x20 * d[2][0] + x21 * d[2][1])
    s23 = d[3][2] - (x20 * d[3][0] + x21 * d[3][1])
    s33 = d[3][3] - (x30 * d[3][0] + x31 * d[3][1])
    inv = 1.0 / (s22 * s33 - s23 * s23)
    y2 = r[2] - (x20 * r[0] + x21 * r[1])
    y3 = r[3] - (x30 * r[0] + x31 * r[1])
    w2 = inv * (s33 * y2 - s23 * y3)
    w3 = inv * (s22 * y3 - s23 * y2)
    w0 = (a0 * r[0] - a1 * r[1]) - (x20 * w2 + x30 * w3)
    w1 = (a2 * r[1] - a1 * r[0]) - (x21 * w2 + x31 * w3)
    return cols, [w0, w1, w2, w3]


def sweep_panels(panels):
    lanes = lax.broadcasted_iota(jnp.int32, panels[0].shape, 1)
    subs = lax.broadcasted_iota(jnp.int32, panels[0].shape, 0)
    for j in range(0, PANEL, 4):
        found = [four_rows(panel, j) for panel in panels]
        out = []
        for panel, (cols, w) in zip(panels, found):
            new = jnp.where((lanes >= j) & (lanes < j + 4), 0.0, panel)
            new = new - ((cols[0] * w[0] + cols[1] * w[1]) + (cols[2] * w[2] + cols[3] * w[3]))
            for m in range(4):
                new = jnp.where(subs == j + m, w[m], new)
            out.append(new)
        panels = out
    return panels


def inverses(mats, work):
    n = mats[0].shape[0]
    count = len(mats)
    for i, mat in enumerate(mats):
        work[i] = mat

    def block(_, carry):
        rows = [work[i, :PANEL, :] for i in range(count)]
        swept = sweep_panels(rows)
        lanes = lax.broadcasted_iota(jnp.int32, (PANEL, n), 1)
        for i in range(count):
            cross = jnp.where(lanes < PANEL, 0.0, rows[i])
            low = work[i, PANEL:, :]
            low_lanes = lax.broadcasted_iota(jnp.int32, low.shape, 1)
            change = mm_tn(cross, swept[i])
            low = jnp.where(low_lanes < PANEL, 0.0, low) - change[PANEL:, :]
            work[i, : n - PANEL, :] = pltpu.roll(low, n - PANEL, 1)
            work[i, n - PANEL :, :] = pltpu.roll(swept[i], n - PANEL, 1)
        return carry

    lax.fori_loop(0, n // PANEL, block, 0)
    return [-work[i] for i in range(count)]


def middle(spread, curv):
    return spread + mm(mm(spread, curv), spread)


def joined_with(first, second, left, mid, y):
    e1, a1, _, p1, _ = first
    e2, a2, c2, p2, b2 = second
    return (
        e1 + mm_tn(a1, mm(mm(e2, left), a1)),
        mm(mm(a2, left), a1),
        c2 + mm_nt(mm(a2, mid), a2),
        p1 + mm(p2 - mm(y, e2), a1),
        b2 + mm_nt(y, a2),
    )


def joined(first, second, inv):
    c1 = first[2]
    left = mm(c1, inv)
    y = mm_nt(first[4] + mm(second[3], c1), left)
    return joined_with(first, second, left, mm(left, c1), y)


def joined_step(first, info, scale, second, inv):
    return joined_with(first, second, inv * scale, inv, mm(info + second[3], inv))


def joined_high(first, second, inv):
    c1 = first[2]
    _, a2, c2, p2, b2 = second
    left = mm(c1, inv)
    y = mm_nt(first[4] + mm(p2, c1), left)
    return c2 + mm_nt(mm(a2, mm(left, c1)), a2), b2 + mm_nt(y, a2)


def joined_low(first, second, inv):
    e1, a1, c1, p1, b1 = first
    e2, p2 = second[0], second[3]
    left = mm(c1, inv)
    y = mm_nt(b1 + mm(p2, c1), left)
    return e1 + mm_tn(a1, mm(mm(e2, left), a1)), p1 + mm(p2 - mm(y, e2), a1)


def put(ref, at, element):
    n = element[0].shape[0]
    ref[at, 0:n, :] = element[0]
    ref[at, n : 2 * n, :] = element[1]
    ref[at, 2 * n : 3 * n, :] = element[2]
    ref[at, 3 * n : 3 * n + 1, :] = element[3]
    ref[at, 3 * n + 1 : 3 * n + 2, :] = element[4]
    ref[at, 3 * n + 2 : 3 * n + 8, :] = jnp.zeros((6, n), jnp.float32)


def get(ref, at):
    n = ref.shape[2]
    return (
        ref[at, 0:n, :],
        ref[at, n : 2 * n, :],
        ref[at, 2 * n : 3 * n, :],
        ref[at, 3 * n : 3 * n + 1, :],
        ref[at, 3 * n + 1 : 3 * n + 2, :],
    )


def transition(kappa, speed):
    n = kappa.shape[1]
    rows = lax.broadcasted_iota(jnp.int32, (n, n), 0)
    cols = lax.broadcasted_iota(jnp.int32, (n, n), 1)
    gap = jnp.where(rows < cols, rows - cols + n, rows - cols)
    turned = jnp.where(gap == 0, 1.0 - 2.0 * kappa, 0.0)
    turned = turned + jnp.where(gap == 1, kappa - 0.5 * speed, 0.0)
    turned = turned + jnp.where(gap == n - 1, kappa + 0.5 * speed, 0.0)
    return turned.T


def local_kernel(place_ref, data_ref, param_ref, locals_ref, agg_ref, work):
    n = param_ref.shape[1]
    steps = (data_ref.shape[0] - 1) // 2
    trans = transition(param_ref[0:1, :], param_ref[1:2, :])
    var = param_ref[2:3, :]
    is_first = place_ref[0] == 0
    is_last = place_ref[0] == place_ref[1] - 1
    cells = data_ref[2 * steps : 2 * steps + 1, :]
    sensors = cells.shape[1]
    states = lax.broadcasted_iota(jnp.int32, (n, sensors), 0).astype(jnp.float32)
    one_hot = jnp.where(states == cells, 1.0, 0.0)
    sums = mm_nt(data_ref[0 : 2 * steps, :], one_hot)
    zero = jnp.zeros((n, n), jnp.float32)
    zero_row = jnp.zeros((1, n), jnp.float32)
    single, infos, scales = [], [], []
    for t in range(steps):
        lam, info = sums[t : t + 1, :], sums[steps + t : steps + t + 1, :]
        damp = 1.0 / (1.0 + var * lam)
        shrink = var * damp
        single.append((
            mm_tn(trans, mm(diag_of(lam * damp), trans)), mm(diag_of(damp), trans),
            diag_of(shrink), mm(info * damp, trans), shrink * info,
        ))
        infos.append(info)
        scales.append(1.0 / var + lam)
    moved_cov = mm_nt(trans * param_ref[4:5, :], trans)
    cov0 = diag_of(var) + jnp.where(is_first, moved_cov, 0.0)
    map0 = jnp.where(is_first, 0.0, trans)
    mean0 = jnp.where(is_first, mm_nt(param_ref[3:4, :], trans), 0.0)
    ahead0 = (zero, map0, cov0, zero_row, mean0)
    lam0 = diag_of(sums[0:1, :])
    e3, _, _, p3, _ = single[3]
    tail = tuple(
        jnp.where(is_last, a, b) for a, b in zip((e3, zero, zero, p3, zero_row), single[3])
    )
    _, s1, s2, s3 = single
    seen = (lam0 + s1[0], s1[1], s1[2], infos[0] + s1[3], s1[4])
    inv0, inv01, m23 = inverses(
        [middle(cov0, lam0), middle(cov0, seen[0]), diag_of(scales[2]) + s3[0]], work
    )
    left = mm(cov0, inv0)
    y = mm_nt(mean0 + mm(infos[0], cov0), left)
    s0 = (
        mm_tn(map0, mm(mm(lam0, left), map0)), mm(left, map0), mm(left, cov0),
        mm(infos[0] - mm(y, lam0), map0), y,
    )
    s01 = joined(ahead0, seen, inv01)
    s23 = joined_step(s2, infos[2], scales[2], s3, m23)
    s23t = joined_step(s2, infos[2], scales[2], tail, m23)
    put(locals_ref, 0, s0)
    put(locals_ref, 1, s01)
    put(locals_ref, 5, s23)
    put(locals_ref, 6, s3)
    found = inverses(
        [middle(s01[2], s2[0]), middle(s01[2], s23[0]), diag_of(scales[1]) + s23[0]], work
    )
    put(locals_ref, 2, joined(s01, s2, found[0]))
    put(locals_ref, 3, joined(s01, s23, found[1]))
    put(locals_ref, 4, joined_step(s1, infos[1], scales[1], s23, found[2]))
    put(agg_ref, 0, joined(s01, s23t, found[1]))


def level_kernel(level, narrow, place_ref, own_ref, other_ref, sides_ref, agg_ref, out_ref, work):
    n = own_ref.shape[2]
    place = place_ref[0]
    span = 1 << level
    upper = (place // span) % 2 == 1
    inside = place % span
    own, other = get(own_ref, 0), get(other_ref, 0)

    def pick(a, b):
        return tuple(jnp.where(upper, x, y) for x, y in zip(a, b))

    low, high = pick(other, own), pick(own, other)
    wanted = [middle(low[2], high[0])]
    if level > 0:
        before, after = get(sides_ref, 0), get(sides_ref, 1)
        alone = jnp.where(upper, inside == 0, inside == span - 1)
        one, two = pick(other, after), pick(before, other)
        unit = jnp.where(eye_mask(n), 1.0, 0.0)
        wanted.append(jnp.where(alone, unit, middle(one[2], two[0])))
    found = inverses(wanted, work)
    agg = joined(low, high, found[0])
    if narrow:
        above = (place // (2 * span)) % 2 == 1
        agg_ref[0:n, :] = jnp.where(above, agg[0], agg[2])
        agg_ref[n : n + 1, :] = jnp.where(above, agg[3], agg[4])
        agg_ref[n + 1 : n + 8, :] = jnp.zeros((7, n), jnp.float32)
    else:
        put(agg_ref, 0, agg)
    if level > 0:
        merged = joined(one, two, found[-1])
        merged = tuple(jnp.where(alone, x, y) for x, y in zip(other, merged))
        put(out_ref, 0, pick(merged, before))
        put(out_ref, 1, pick(after, merged))
    else:
        empty = tuple(jnp.zeros_like(x) for x in other)
        put(out_ref, 0, pick(other, empty))
        put(out_ref, 1, pick(empty, other))


def last_level(place, span, other_ref, sides_ref, work):
    n = other_ref.shape[1]
    upper = (place // span) % 2 == 1
    inside = place % span
    alone = jnp.where(upper, inside == 0, inside == span - 1)
    before, after = get(sides_ref, 0), get(sides_ref, 1)
    mat, vec = other_ref[0:n, :], other_ref[n : n + 1, :]
    unit = jnp.where(eye_mask(n), 1.0, 0.0)
    c1 = jnp.where(upper, mat, after[2])
    e2 = jnp.where(upper, before[0], mat)
    b1 = jnp.where(upper, vec, after[4])
    p2 = jnp.where(upper, before[3], vec)
    inv = inverses([jnp.where(alone, unit, middle(c1, e2))], work)[0]
    left = mm(c1, inv)
    y = mm_nt(b1 + mm(p2, c1), left)
    link = jnp.where(upper, before[1].T, after[1])
    core = jnp.where(upper, mm(left, c1), mm(e2, left))
    y = jnp.where(upper, y, p2 - mm(y, e2))
    new = jnp.where(upper, before[2], after[0]) + mm_tn(link, mm(core, link))
    row = jnp.where(upper, before[4], after[3]) + mm(y, link)
    new, row = jnp.where(alone, mat, new), jnp.where(alone, vec, row)
    before = (None, None, jnp.where(upper, new, before[2]), None, jnp.where(upper, row, before[4]))
    after = (jnp.where(upper, after[0], new), None, None, jnp.where(upper, after[3], row), None)
    return before, after


def final_kernel(span, place_ref, locals_ref, other_ref, sides_ref, mean_ref, smooth_ref, var_ref, work):
    n = locals_ref.shape[2]
    is_first = place_ref[0] == 0
    unit = jnp.where(eye_mask(n), 1.0, 0.0)
    before, after = last_level(place_ref[0], span, other_ref, sides_ref, work)
    before = (None, None, jnp.where(is_first, unit, before[2]), None, before[4])
    ahead = [get(locals_ref, i) for i in range(4)]
    behind = [get(locals_ref, i) for i in range(4, 7)]
    found = inverses(
        [middle(before[2], a[0]) for a in ahead] + [middle(b[2], after[0]) for b in behind], work
    )
    states = [joined_high(before, a, inv) for a, inv in zip(ahead, found[:4])]
    later = [joined_low(b, after, inv) for b, inv in zip(behind, found[4:])]
    later.append((after[0], after[3]))
    found = inverses([middle(s[0], l[0]) for s, l in zip(states, later)], work)
    diagonal = eye_mask(n)
    for t, ((cov, mean), (_, row)) in enumerate(zip(states, later)):
        left = mm(cov, found[t])
        mean_ref[t : t + 1, :] = mean
        smooth_ref[t : t + 1, :] = mm_nt(mean + mm(row, cov), left)
        var_ref[t : t + 1, :] = jnp.sum(
            jnp.where(diagonal, mm(left, cov), 0.0), axis=0, keepdims=True
        )


def run(kernel, shapes, works, operands, n, scalars=1):
    specs = [pl.BlockSpec(memory_space=pltpu.SMEM)] * scalars
    specs += [pl.BlockSpec(memory_space=pltpu.VMEM)] * (len(operands) - scalars)
    single = not isinstance(shapes, list)
    outs = pl.BlockSpec(memory_space=pltpu.VMEM)
    return pl.pallas_call(
        kernel,
        out_shape=shapes,
        in_specs=specs,
        out_specs=outs if single else [outs] * len(shapes),
        scratch_shapes=[pltpu.VMEM((works, n, n), jnp.float32)],
        compiler_params=pltpu.CompilerParams(vmem_limit_bytes=40 * 2**20),
    )(*operands)


def local(readings, present, cell_of, noise_var, kappa, speed, process_var, prior_mean, prior_var):
    n = kappa.shape[0]
    outer, steps, sensors = readings.shape
    blocks = lax.axis_size("ta") * lax.axis_size("au")
    place = lax.axis_index("ta") * lax.axis_size("au") + lax.axis_index("au")
    where = jnp.stack([place, jnp.full_like(place, blocks)]).astype(jnp.int32)
    weight = present.astype(jnp.float32) / noise_var
    cells = jnp.broadcast_to(cell_of.astype(jnp.float32), (outer, 1, sensors))
    sent = jnp.concatenate([weight, weight * readings, cells], axis=1)
    data = lax.all_to_all(sent, "ta", split_axis=0, concat_axis=0, tiled=True)
    data = jnp.swapaxes(data, 0, 1).reshape(2 * steps + 1, outer * sensors)

    params = jnp.stack([kappa, speed, process_var, prior_mean, prior_var])

    def elements(count):
        return jax.ShapeDtypeStruct((count, 3 * n + 8, n), jnp.float32)

    pieces, agg = run(
        local_kernel, [elements(7), elements(1)], 4,
        [where, data, params], n,
    )
    sides = jnp.zeros((2, 3 * n + 8, n), jnp.float32)
    levels = blocks.bit_length() - 1
    for level in range(levels):
        pairs = [(i, i ^ (1 << level)) for i in range(blocks)]
        other = lax.ppermute(agg, ("ta", "au"), pairs)
        if level == levels - 1:
            break
        narrow = level == levels - 2
        sent = jax.ShapeDtypeStruct((n + 8, n), jnp.float32) if narrow else elements(1)
        agg, sides = run(
            functools.partial(level_kernel, level, narrow),
            [sent, elements(2)], 2, [where, agg, other, sides], n,
        )
    row = jax.ShapeDtypeStruct((steps, n), jnp.float32)
    return tuple(
        run(
            functools.partial(final_kernel, blocks // 2),
            [row, row, row], 8, [where, pieces, other, sides], n,
        )
    )


def solution(mesh):
    placed = (
        P("grp", "au", "ta"),
        P("grp", "au", "ta"),
        P("ta"),
        P("ta"),
        P(),
        P(),
        P(),
        P("grp"),
        P(),
    )
    out = P(("grp", "ta", "au"), None)
    return jax.shard_map(
        local, mesh=mesh, in_specs=placed, out_specs=(out, out, out), check_vma=False
    )
```

```python
import functools

import jax
import jax.numpy as jnp
from jax import lax
from jax.experimental import pallas as pl
from jax.experimental.pallas import tpu as pltpu
from jax.sharding import PartitionSpec as P

HIGHEST = lax.Precision.HIGHEST
PANEL = 32


def mm(a, b):
    return lax.dot_general(
        a, b, (((1,), (0,)), ((), ())), precision=HIGHEST, preferred_element_type=jnp.float32
    )


def mm_nt(a, b):
    return lax.dot_general(
        a, b, (((1,), (1,)), ((), ())), precision=HIGHEST, preferred_element_type=jnp.float32
    )


def mm_tn(a, b):
    return lax.dot_general(
        a, b, (((0,), (0,)), ((), ())), precision=HIGHEST, preferred_element_type=jnp.float32
    )


def eye_mask(n):
    return lax.broadcasted_iota(jnp.int32, (n, n), 0) == lax.broadcasted_iota(
        jnp.int32, (n, n), 1
    )


def diag_of(row):
    n = row.shape[1]
    return jnp.where(eye_mask(n), jnp.broadcast_to(row, (n, n)), 0.0)


def four_rows(panel, j):
    rows, n = panel.shape
    row_lanes = lax.broadcasted_iota(jnp.int32, (1, n), 1)
    cols = [jnp.broadcast_to(panel[:, j + m : j + m + 1], (rows, n)) for m in range(4)]
    d = [[cols[m][j + i : j + i + 1, :] for m in range(4)] for i in range(4)]
    r = []
    for i in range(4):
        row = jnp.where((row_lanes >= j) & (row_lanes < j + 4), 0.0, panel[j + i : j + i + 1, :])
        r.append(jnp.where(row_lanes == j + i, -1.0, row))
    inv = 1.0 / (d[0][0] * d[1][1] - d[1][0] * d[1][0])
    a0, a1, a2 = d[1][1] * inv, d[1][0] * inv, d[0][0] * inv
    x20, x21 = d[2][0] * a0 - d[2][1] * a1, d[2][1] * a2 - d[2][0] * a1
    x30, x31 = d[3][0] * a0 - d[3][1] * a1, d[3][1] * a2 - d[3][0] * a1
    s22 = d[2][2] - (x20 * d[2][0] + x21 * d[2][1])
    s23 = d[3][2] - (x20 * d[3][0] + x21 * d[3][1])
    s33 = d[3][3] - (x30 * d[3][0] + x31 * d[3][1])
    inv = 1.0 / (s22 * s33 - s23 * s23)
    y2 = r[2] - (x20 * r[0] + x21 * r[1])
    y3 = r[3] - (x30 * r[0] + x31 * r[1])
    w2 = inv * (s33 * y2 - s23 * y3)
    w3 = inv * (s22 * y3 - s23 * y2)
    w0 = (a0 * r[0] - a1 * r[1]) - (x20 * w2 + x30 * w3)
    w1 = (a2 * r[1] - a1 * r[0]) - (x21 * w2 + x31 * w3)
    return cols, [w0, w1, w2, w3]


def sweep_panels(panels):
    lanes = lax.broadcasted_iota(jnp.int32, panels[0].shape, 1)
    subs = lax.broadcasted_iota(jnp.int32, panels[0].shape, 0)
    for j in range(0, PANEL, 4):
        found = [four_rows(panel, j) for panel in panels]
        out = []
        for panel, (cols, w) in zip(panels, found):
            new = jnp.where((lanes >= j) & (lanes < j + 4), 0.0, panel)
            new = new - ((cols[0] * w[0] + cols[1] * w[1]) + (cols[2] * w[2] + cols[3] * w[3]))
            for m in range(4):
                new = jnp.where(subs == j + m, w[m], new)
            out.append(new)
        panels = out
    return panels


def inverses(mats, work):
    n = mats[0].shape[0]
    count = len(mats)
    for i, mat in enumerate(mats):
        work[i] = mat

    def block(_, carry):
        rows = [work[i, :PANEL, :] for i in range(count)]
        swept = sweep_panels(rows)
        lanes = lax.broadcasted_iota(jnp.int32, (PANEL, n), 1)
        for i in range(count):
            cross = jnp.where(lanes < PANEL, 0.0, rows[i])
            low = work[i, PANEL:, :]
            low_lanes = lax.broadcasted_iota(jnp.int32, low.shape, 1)
            change = mm_tn(cross, swept[i])
            low = jnp.where(low_lanes < PANEL, 0.0, low) - change[PANEL:, :]
            work[i, : n - PANEL, :] = pltpu.roll(low, n - PANEL, 1)
            work[i, n - PANEL :, :] = pltpu.roll(swept[i], n - PANEL, 1)
        return carry

    lax.fori_loop(0, n // PANEL, block, 0)
    return [-work[i] for i in range(count)]


def middle(spread, curv):
    return spread + mm(mm(spread, curv), spread)


def joined_with(first, second, left, mid, y):
    e1, a1, _, p1, _ = first
    e2, a2, c2, p2, b2 = second
    return (
        e1 + mm_tn(a1, mm(mm(e2, left), a1)),
        mm(mm(a2, left), a1),
        c2 + mm_nt(mm(a2, mid), a2),
        p1 + mm(p2 - mm(y, e2), a1),
        b2 + mm_nt(y, a2),
    )


def joined(first, second, inv):
    c1 = first[2]
    left = mm(c1, inv)
    y = mm_nt(first[4] + mm(second[3], c1), left)
    return joined_with(first, second, left, mm(left, c1), y)


def joined_step(first, info, scale, second, inv):
    return joined_with(first, second, inv * scale, inv, mm(info + second[3], inv))


def joined_high(first, second, inv):
    c1 = first[2]
    _, a2, c2, p2, b2 = second
    left = mm(c1, inv)
    y = mm_nt(first[4] + mm(p2, c1), left)
    return c2 + mm_nt(mm(a2, mm(left, c1)), a2), b2 + mm_nt(y, a2)


def joined_low(first, second, inv):
    e1, a1, c1, p1, b1 = first
    e2, p2 = second[0], second[3]
    left = mm(c1, inv)
    y = mm_nt(b1 + mm(p2, c1), left)
    return e1 + mm_tn(a1, mm(mm(e2, left), a1)), p1 + mm(p2 - mm(y, e2), a1)


def put(ref, at, element):
    n = element[0].shape[0]
    ref[at, 0:n, :] = element[0]
    ref[at, n : 2 * n, :] = element[1]
    ref[at, 2 * n : 3 * n, :] = element[2]
    ref[at, 3 * n : 3 * n + 1, :] = element[3]
    ref[at, 3 * n + 1 : 3 * n + 2, :] = element[4]
    ref[at, 3 * n + 2 : 3 * n + 8, :] = jnp.zeros((6, n), jnp.float32)


def get(ref, at):
    n = ref.shape[2]
    return (
        ref[at, 0:n, :],
        ref[at, n : 2 * n, :],
        ref[at, 2 * n : 3 * n, :],
        ref[at, 3 * n : 3 * n + 1, :],
        ref[at, 3 * n + 1 : 3 * n + 2, :],
    )


def first_kernel(cov_ref, out_ref, work):
    out_ref[...] = inverses([cov_ref[...]], work)[0]


def local_kernel(place_ref, data_ref, trans_ref, q_ref, first_ref, prior_ref,
                 locals_ref, agg_ref, work):
    n = trans_ref.shape[0]
    steps = (data_ref.shape[0] - 1) // 2
    trans = trans_ref[...]
    var = q_ref[...]
    is_first = place_ref[0] == 0
    is_last = place_ref[0] == place_ref[1] - 1
    cells = data_ref[2 * steps : 2 * steps + 1, :]
    sensors = cells.shape[1]
    states = lax.broadcasted_iota(jnp.int32, (n, sensors), 0).astype(jnp.float32)
    one_hot = jnp.where(states == cells, 1.0, 0.0)
    sums = mm_nt(data_ref[0 : 2 * steps, :], one_hot)
    zero = jnp.zeros((n, n), jnp.float32)
    zero_row = jnp.zeros((1, n), jnp.float32)
    single, infos, scales = [], [], []
    for t in range(steps):
        lam, info = sums[t : t + 1, :], sums[steps + t : steps + t + 1, :]
        damp = 1.0 / (1.0 + var * lam)
        shrink = var * damp
        single.append((
            mm_tn(trans, mm(diag_of(lam * damp), trans)), mm(diag_of(damp), trans),
            diag_of(shrink), mm(info * damp, trans), shrink * info,
        ))
        infos.append(info)
        scales.append(1.0 / var + lam)
    known = first_ref[...]
    moved = mm_nt(prior_ref[...], trans)
    known_info = infos[0] + mm(moved, known)
    info0 = jnp.where(is_first, known_info, infos[0])
    high0 = jnp.where(is_first, known + diag_of(sums[0:1, :]), diag_of(scales[0]))
    e3, _, _, p3, _ = single[3]
    tail = tuple(
        jnp.where(is_last, a, b) for a, b in zip((e3, zero, zero, p3, zero_row), single[3])
    )
    s0, s1, s2, s3 = single
    m0, m01, m23 = inverses([high0, high0 + s1[0], diag_of(scales[2]) + s3[0]], work)
    head = (zero, zero, m0, zero_row, mm(info0, m0))
    s0 = tuple(jnp.where(is_first, a, b) for a, b in zip(head, s0))
    s01 = joined_step(s0, info0, scales[0], s1, m01)
    s23 = joined_step(s2, infos[2], scales[2], s3, m23)
    s23t = joined_step(s2, infos[2], scales[2], tail, m23)
    put(locals_ref, 0, s0)
    put(locals_ref, 1, s01)
    put(locals_ref, 5, s23)
    put(locals_ref, 6, s3)
    found = inverses(
        [middle(s01[2], s2[0]), middle(s01[2], s23[0]), diag_of(scales[1]) + s23[0]], work
    )
    put(locals_ref, 2, joined(s01, s2, found[0]))
    put(locals_ref, 3, joined(s01, s23, found[1]))
    put(locals_ref, 4, joined_step(s1, infos[1], scales[1], s23, found[2]))
    put(agg_ref, 0, joined(s01, s23t, found[1]))


def level_kernel(level, narrow, place_ref, own_ref, other_ref, sides_ref, agg_ref, out_ref, work):
    n = own_ref.shape[2]
    place = place_ref[0]
    span = 1 << level
    upper = (place // span) % 2 == 1
    inside = place % span
    own, other = get(own_ref, 0), get(other_ref, 0)

    def pick(a, b):
        return tuple(jnp.where(upper, x, y) for x, y in zip(a, b))

    low, high = pick(other, own), pick(own, other)
    wanted = [middle(low[2], high[0])]
    if level > 0:
        before, after = get(sides_ref, 0), get(sides_ref, 1)
        alone = jnp.where(upper, inside == 0, inside == span - 1)
        one, two = pick(other, after), pick(before, other)
        unit = jnp.where(eye_mask(n), 1.0, 0.0)
        wanted.append(jnp.where(alone, unit, middle(one[2], two[0])))
    found = inverses(wanted, work)
    agg = joined(low, high, found[0])
    if narrow:
        above = (place // (2 * span)) % 2 == 1
        agg_ref[0:n, :] = jnp.where(above, agg[0], agg[2])
        agg_ref[n : n + 1, :] = jnp.where(above, agg[3], agg[4])
        agg_ref[n + 1 : n + 8, :] = jnp.zeros((7, n), jnp.float32)
    else:
        put(agg_ref, 0, agg)
    if level > 0:
        merged = joined(one, two, found[-1])
        merged = tuple(jnp.where(alone, x, y) for x, y in zip(other, merged))
        put(out_ref, 0, pick(merged, before))
        put(out_ref, 1, pick(after, merged))
    else:
        empty = tuple(jnp.zeros_like(x) for x in other)
        put(out_ref, 0, pick(other, empty))
        put(out_ref, 1, pick(empty, other))


def last_level(place, span, other_ref, sides_ref, work):
    n = other_ref.shape[1]
    upper = (place // span) % 2 == 1
    inside = place % span
    alone = jnp.where(upper, inside == 0, inside == span - 1)
    before, after = get(sides_ref, 0), get(sides_ref, 1)
    mat, vec = other_ref[0:n, :], other_ref[n : n + 1, :]
    unit = jnp.where(eye_mask(n), 1.0, 0.0)
    c1 = jnp.where(upper, mat, after[2])
    e2 = jnp.where(upper, before[0], mat)
    b1 = jnp.where(upper, vec, after[4])
    p2 = jnp.where(upper, before[3], vec)
    inv = inverses([jnp.where(alone, unit, middle(c1, e2))], work)[0]
    left = mm(c1, inv)
    y = mm_nt(b1 + mm(p2, c1), left)
    link = jnp.where(upper, before[1].T, after[1])
    core = jnp.where(upper, mm(left, c1), mm(e2, left))
    y = jnp.where(upper, y, p2 - mm(y, e2))
    new = jnp.where(upper, before[2], after[0]) + mm_tn(link, mm(core, link))
    row = jnp.where(upper, before[4], after[3]) + mm(y, link)
    new, row = jnp.where(alone, mat, new), jnp.where(alone, vec, row)
    before = (None, None, jnp.where(upper, new, before[2]), None, jnp.where(upper, row, before[4]))
    after = (jnp.where(upper, after[0], new), None, None, jnp.where(upper, after[3], row), None)
    return before, after


def final_kernel(span, place_ref, locals_ref, other_ref, sides_ref, mean_ref, smooth_ref, var_ref, work):
    n = locals_ref.shape[2]
    is_first = place_ref[0] == 0
    unit = jnp.where(eye_mask(n), 1.0, 0.0)
    before, after = last_level(place_ref[0], span, other_ref, sides_ref, work)
    before = (None, None, jnp.where(is_first, unit, before[2]), None, before[4])
    ahead = [get(locals_ref, i) for i in range(4)]
    behind = [get(locals_ref, i) for i in range(4, 7)]
    found = inverses(
        [middle(before[2], a[0]) for a in ahead] + [middle(b[2], after[0]) for b in behind], work
    )
    states = [joined_high(before, a, inv) for a, inv in zip(ahead, found[:4])]
    later = [joined_low(b, after, inv) for b, inv in zip(behind, found[4:])]
    later.append((after[0], after[3]))
    found = inverses([middle(s[0], l[0]) for s, l in zip(states, later)], work)
    for t, ((cov, mean), (_, row)) in enumerate(zip(states, later)):
        turned = mm(found[t], cov)
        mean_ref[t : t + 1, :] = mean
        smooth_ref[t : t + 1, :] = mm(mean + mm(row, cov), turned)
        var_ref[t : t + 1, :] = jnp.sum(turned * cov, axis=0, keepdims=True)


def run(kernel, shapes, works, operands, n, scalars=1):
    specs = [pl.BlockSpec(memory_space=pltpu.SMEM)] * scalars
    specs += [pl.BlockSpec(memory_space=pltpu.VMEM)] * (len(operands) - scalars)
    single = not isinstance(shapes, list)
    outs = pl.BlockSpec(memory_space=pltpu.VMEM)
    return pl.pallas_call(
        kernel,
        out_shape=shapes,
        in_specs=specs,
        out_specs=outs if single else [outs] * len(shapes),
        scratch_shapes=[pltpu.VMEM((works, n, n), jnp.float32)],
        compiler_params=pltpu.CompilerParams(vmem_limit_bytes=40 * 2**20),
    )(*operands)


def transition(kappa, speed):
    n = kappa.shape[0]
    rows = jnp.arange(n)[:, None]
    cols = jnp.arange(n)[None, :]
    ahead = (cols == (rows + 1) % n).astype(jnp.float32)
    behind = (cols == (rows - 1) % n).astype(jnp.float32)
    center = (cols == rows).astype(jnp.float32)
    return (
        center * (1.0 - 2.0 * kappa)[:, None]
        + ahead * (kappa - 0.5 * speed)[:, None]
        + behind * (kappa + 0.5 * speed)[:, None]
    )


def local(readings, present, cell_of, noise_var, kappa, speed, process_var, prior_mean, prior_var):
    n = kappa.shape[0]
    outer, steps, sensors = readings.shape
    blocks = lax.axis_size("ta") * lax.axis_size("au")
    place = lax.axis_index("ta") * lax.axis_size("au") + lax.axis_index("au")
    where = jnp.stack([place, jnp.full_like(place, blocks)]).astype(jnp.int32)
    weight = present.astype(jnp.float32) / noise_var
    cells = jnp.broadcast_to(cell_of.astype(jnp.float32), (outer, 1, sensors))
    sent = jnp.concatenate([weight, weight * readings, cells], axis=1)
    data = lax.all_to_all(sent, "ta", split_axis=0, concat_axis=0, tiled=True)
    data = jnp.swapaxes(data, 0, 1).reshape(2 * steps + 1, outer * sensors)

    trans = transition(kappa, speed)
    start = jnp.matmul(trans * prior_var[None, :], trans.T, precision=HIGHEST)
    start = start + jnp.diag(process_var)
    mat = jax.ShapeDtypeStruct((n, n), jnp.float32)
    known = run(first_kernel, mat, 1, [start], n, 0)

    def elements(count):
        return jax.ShapeDtypeStruct((count, 3 * n + 8, n), jnp.float32)

    pieces, agg = run(
        local_kernel, [elements(7), elements(1)], 4,
        [where, data, trans, process_var[None, :], known, prior_mean[None, :]], n,
    )
    sides = jnp.zeros((2, 3 * n + 8, n), jnp.float32)
    levels = blocks.bit_length() - 1
    for level in range(levels):
        pairs = [(i, i ^ (1 << level)) for i in range(blocks)]
        other = lax.ppermute(agg, ("ta", "au"), pairs)
        if level == levels - 1:
            break
        narrow = level == levels - 2
        sent = jax.ShapeDtypeStruct((n + 8, n), jnp.float32) if narrow else elements(1)
        agg, sides = run(
            functools.partial(level_kernel, level, narrow),
            [sent, elements(2)], 2, [where, agg, other, sides], n,
        )
    row = jax.ShapeDtypeStruct((steps, n), jnp.float32)
    return tuple(
        run(
            functools.partial(final_kernel, blocks // 2),
            [row, row, row], 8, [where, pieces, other, sides], n,
        )
    )


def solution(mesh):
    placed = (
        P("grp", "au", "ta"),
        P("grp", "au", "ta"),
        P("ta"),
        P("ta"),
        P(),
        P(),
        P(),
        P("grp"),
        P(),
    )
    out = P(("grp", "ta", "au"), None)
    return jax.shard_map(
        local, mesh=mesh, in_specs=placed, out_specs=(out, out, out), check_vma=False
    )
```
